32 devices in a mesh: pair: 8 (over y, x, core), col: 4 (over z).
Axes of the slice: x: 2, y: 2, z: 4, core: 2. Of those that a mesh axis runs over, the one named last changes fastest.
Arguments:
- tmatrix: bfloat16 [8, 2, 4096, 4096], P('pair', None, None, 'col'), may hold values from -0.046875 to 0.046875
- translation: bfloat16 [8, 2, 4096, 4096], P('pair', None, None, 'col'), may hold values from -0.0625 to 0.0625
- incident: bfloat16 [8, 4096, 256], P('pair', 'col'), may hold values from -6 to 6
- farfield: bfloat16 [2, 2048, 4096], P(None, None, 'col'), may hold values from -0.0625 to 0.0625
- centres: int32 [8, 3], replicated, may hold values from -8 to 8
Outputs:
- amplitude: float32 [8, 2048, 128], P('pair', 'col')
The draws below stay inside these ranges and needn't reach their ends.
All inputs are finite; a program needn't handle non-finite values.
Results may differ from the reference program's by a relative error of at most 0.034.
Values may be sent and summed in bfloat16 or wider, within the bound.
A program may use at most 128 MiB of HBM per device.

```python
import math
import jax
import jax.numpy as jnp
from jax import lax

M = 4096
K = 128
S = 2048
ITERS = 3
LEVEL = 2
MC = 1024
KH = 64
CLUSTERS = 8
N_COL = 4


def set_ends(entries, stream_key, least, high):
    dims = entries.shape
    spot = [jax.random.randint(jax.random.fold_in(stream_key, axis), (), 0, dims[axis]) for axis in range(len(dims))]
    entries = entries.at[tuple(spot)].set(least)
    longest = dims.index(max(dims))
    spot[longest] = (spot[longest] + 1) % dims[longest]
    return entries.at[tuple(spot)].set(high)


def level_of(own_key, dims, cuts, low, high):
    level = 1.0
    for position, parts in cuts:
        steps = jax.random.uniform(jax.random.fold_in(jax.random.fold_in(own_key, 6), position), (parts,), jnp.float32, low / len(cuts), high / len(cuts))
        level = level * jnp.repeat(jnp.exp(steps), dims[position] // parts).reshape((-1,) + (1,) * (len(dims) - 1 - position))
    return level


def normal_values(own_key, shape, width, bound, cuts=(), held_as=jnp.bfloat16):
    entries = jax.random.normal(own_key, shape, jnp.float32) * width
    if len(cuts) > 0:
        entries = level_of(own_key, shape, cuts, -0.22, 0.18) * entries
    return jnp.clip(entries, min=-bound, max=bound).astype(held_as)


def setup_inputs(seed: int = 0) -> dict:
    streams_of = jax.random.split(jax.random.key(seed), 6)
    return {
        "tmatrix": normal_values(streams_of[0], (CLUSTERS, 2, M, M), (4 * M) ** -0.5, 0.046875, ((0, 8), (3, 4))),
        "translation": normal_values(streams_of[1], (CLUSTERS, 2, M, M), (2 * M) ** -0.5, 0.0625, ((0, 8), (3, 4))),
        "incident": normal_values(streams_of[2], (CLUSTERS, M, 2 * K), 1.0, 6.0, ((0, 8), (1, 4))),
        "farfield": normal_values(streams_of[3], (2, S, M), (2 * M) ** -0.5, 0.0625, ((2, 4),)),
        "centres": set_ends(jax.random.randint(streams_of[4], (CLUSTERS, 3), -8, 9), jax.random.fold_in(streams_of[4], 1), -8, 8).astype(jnp.int32),
    }


def turned_block(vector):
    half_width = vector.shape[1] // 2
    return jnp.concatenate([-vector[:, half_width:], vector[:, :half_width]], axis=1)


def panel_sum(matrix, vector):
    turned = turned_block(vector)
    total = jnp.zeros((matrix.shape[1], vector.shape[1]), jnp.float32)
    for block_index in range(N_COL):
        offset = block_index * MC
        partial_term = jnp.dot(matrix[0][:, offset:offset + MC], vector[offset:offset + MC], preferred_element_type=jnp.float32)
        partial_term = partial_term + jnp.dot(matrix[1][:, offset:offset + MC], turned[offset:offset + MC], preferred_element_type=jnp.float32)
        rounded = lax.optimization_barrier(partial_term.astype(jnp.bfloat16))
        total = total + rounded.astype(jnp.float32)
    return total


def direction_phase(centre):
    steps_int = jnp.arange(S, dtype=jnp.int32)
    polar = (math.pi / S) * (steps_int.astype(jnp.float32) + 0.5)
    azimuth = (2.0 * math.pi / 97.0) * ((steps_int * 40) % 97).astype(jnp.float32)
    spot = centre.astype(jnp.float32)
    return 0.7 * (jnp.sin(polar) * jnp.cos(azimuth) * spot[0] + jnp.sin(polar) * jnp.sin(azimuth) * spot[1] + jnp.cos(polar) * spot[2])


def rotate(field, phase):
    half_width = field.shape[1] // 2
    cosine = jnp.cos(phase)[:, None]
    sine = jnp.sin(phase)[:, None]
    real_part = field[:, :half_width]
    imag_part = field[:, half_width:]
    return jnp.concatenate([cosine * real_part + sine * imag_part, cosine * imag_part - sine * real_part], axis=1)


def far_field(farfield, coeffs):
    return jnp.dot(farfield[0], coeffs, preferred_element_type=jnp.float32) + jnp.dot(farfield[1], turned_block(coeffs), preferred_element_type=jnp.float32)


def reference(tmatrix, translation, incident, farfield, centres):
    coeffs = [panel_sum(tmatrix[member], incident[member]).astype(jnp.bfloat16) for member in range(CLUSTERS)]
    for iteration in range(ITERS):
        fresh = []
        for member in range(CLUSTERS):
            other = member ^ (1 << LEVEL)
            driven = (incident[member].astype(jnp.float32) + panel_sum(translation[member], coeffs[other])).astype(jnp.bfloat16)
            fresh.append(panel_sum(tmatrix[member], driven).astype(jnp.bfloat16))
        coeffs = fresh
    rotated = [rotate(far_field(farfield, coeffs[member]), direction_phase(centres[member])) for member in range(CLUSTERS)]
    outputs = []
    for member in range(CLUSTERS):
        merged = rotated[member] + rotated[member ^ (1 << LEVEL)]
        column_half = (member >> LEVEL) & 1
        outputs.append(jnp.concatenate([merged[:, column_half * KH:(column_half + 1) * KH], merged[:, K + column_half * KH:K + (column_half + 1) * KH]], axis=1))
    return jnp.stack(outputs)
```

```python
import functools
import math

import jax
import jax.numpy as jnp
from jax import lax
from jax.experimental import pallas as pl
from jax.experimental.pallas import tpu as pltpu
from jax.sharding import PartitionSpec as P

ITERS = 3
LEVEL = 2
MESH = pl.DeviceIdType.MESH
BF16 = jnp.bfloat16
F32 = jnp.float32
CHUNKS = 4
LAG = 2


def direction_phase(centre, total_rows):
    steps_int = jnp.arange(total_rows, dtype=jnp.int32)
    polar = math.pi / total_rows * (steps_int.astype(F32) + 0.5)
    azimuth = 2.0 * math.pi / 97.0 * (steps_int * 40 % 97).astype(F32)
    spot = centre.astype(F32)
    return 0.7 * (
        jnp.sin(polar) * jnp.cos(azimuth) * spot[0]
        + jnp.sin(polar) * jnp.sin(azimuth) * spot[1]
        + jnp.cos(polar) * spot[2]
    )


def dot(a, b):
    return jnp.dot(a, b, preferred_element_type=F32)


def kernel(
    n, tm, tr, ff, e_ref, cos_ref, sin_ref, out_ref,
    w, f, xs, xsrc, abuf, part, recv, fpart, frecv,
    wsem, fsem, ssem, rsem, psem, qsem, fssem, frsem,
):
    Q = CHUNKS
    c = lax.axis_index("col")
    g = lax.axis_index("pair")
    half = (g // 2**LEVEL) % 2
    other = g + 2**LEVEL * (1 - 2 * half)
    rows, width = e_ref.shape
    full = width // 2
    cr = rows // Q
    fr = out_ref.shape[0] // Q
    sends = (n - 1) * Q

    n_right, n_left = n - 1 - c, c
    prim_right = n_right > n_left
    n_sec = jnp.minimum(n_right, n_left) * Q

    def step(i):
        k = jnp.maximum(i - LAG, 0)
        mid = (i >= LAG) & (k < 2 * n_sec)
        sec = mid & (k % 2 == 0)
        pri_idx = jnp.where(i < LAG, i, jnp.where(mid, LAG + k // 2, i - n_sec))
        idx = jnp.where(sec, k // 2, pri_idx)
        right = jnp.where(sec, jnp.where(prim_right, 0, 1), jnp.where(prim_right, 1, 0))
        j, q = idx // Q, idx % Q
        d = jnp.where(right == 1, n - 1 - j, j)
        target = jnp.where(right == 1, c + 1, c - 1)
        has_in = jnp.where(right == 1, c > 0, c < n - 1)
        slot_out = jnp.where((right == 0) & (d == target), n, d)
        return d, q, target, has_in, slot_out

    def order(i):
        own = i >= sends
        d, q, _, _, _ = step(jnp.minimum(i, sends - 1))
        return jnp.where(own, c, d), jnp.where(own, i - sends, q)

    def w_copy(which, i):
        d, q = order(i)
        src = tm if which == 0 else tr
        at = pl.ds(pl.multiple_of(d * rows + q * cr, cr), cr)
        return pltpu.make_async_copy(src.at[0, :, at, :], w.at[which, :, at, :], wsem.at[which, i])

    for which in range(2):

        def load(i, _, which=which):
            w_copy(which, i).start()
            return 0

        lax.fori_loop(0, n * Q, load, 0)
    f_copy = pltpu.make_async_copy(ff, f, fsem)
    f_copy.start()

    barrier = pltpu.get_barrier_semaphore()

    @pl.when(c > 0)
    def _():
        pl.semaphore_signal(barrier, inc=1, device_id={"col": c - 1}, device_id_type=MESH)

    @pl.when(c < n - 1)
    def _():
        pl.semaphore_signal(barrier, inc=1, device_id={"col": c + 1}, device_id_type=MESH)

    pl.semaphore_signal(barrier, inc=1, device_id={"pair": other}, device_id_type=MESH)
    pl.semaphore_wait(
        barrier, 1 + jnp.where(c > 0, 1, 0) + jnp.where(c < n - 1, 1, 0)
    )

    def send_copy(par, i, d, q, target, slot_out):
        return pltpu.make_async_remote_copy(
            src_ref=part.at[par, d, q],
            dst_ref=recv.at[par, slot_out, q],
            send_sem=ssem.at[par, i],
            recv_sem=rsem.at[par, slot_out, q],
            device_id={"col": target},
            device_id_type=MESH,
        )

    def arrived(par, slot, q):
        pltpu.make_async_copy(
            recv.at[par, slot, q], recv.at[par, slot, q], rsem.at[par, slot, q]
        ).wait()

    def pair_copy(ex, q):
        at = pl.ds(pl.multiple_of(q * cr, cr), cr)
        return pltpu.make_async_remote_copy(
            src_ref=abuf.at[at, :],
            dst_ref=xsrc.at[ex % 2, at, :],
            send_sem=psem.at[ex % 2, q],
            recv_sem=qsem.at[ex % 2, q],
            device_id={"pair": other},
            device_id_type=MESH,
        )

    def turn(x):
        xs[0:rows, :] = x
        xs[rows : 2 * rows, 0:full] = -x[:, full:]
        xs[rows : 2 * rows, full:] = x[:, :full]

    def product(which, d, q):
        at = pl.ds(pl.multiple_of(d * rows + q * cr, cr), cr)
        return dot(w[which, 0, at, :], xs[0:rows, :]) + dot(w[which, 1, at, :], xs[rows:, :])

    xsrc[2] = e_ref[...]

    def one_product(p, _):
        which = p % 2
        par = p % 2
        ex = p // 2

        @pl.when(which == 1)
        def _():
            def wait_pair(q, _):
                pair_copy(ex, q).wait()
                return 0

            lax.fori_loop(0, Q, wait_pair, 0)
            turn(xsrc[ex % 2])

        @pl.when(which == 0)
        def _():
            turn(xsrc[2])

        def loaded(i):
            @pl.when(p == 0)
            def _():
                w_copy(0, i).wait()

            @pl.when(p == 1)
            def _():
                w_copy(1, i).wait()

        def send_step(i, _):
            d, q, target, has_in, slot_out = step(i)
            loaded(i)
            value = product(which, d, q)
            copy = send_copy(par, i, d, q, target, slot_out)

            @pl.when(p >= 2)
            def _():
                copy.wait_send()

            @pl.when(has_in)
            def _():
                arrived(par, d, q)
                part[par, d, q] = (value + recv[par, d, q].astype(F32)).astype(BF16)

            @pl.when(jnp.logical_not(has_in))
            def _():
                part[par, d, q] = value.astype(BF16)

            copy.start()
            return 0

        lax.fori_loop(0, sends, send_step, 0)

        def own_step(q, _):
            loaded(sends + q)
            at = pl.ds(pl.multiple_of(q * cr, cr), cr)
            value = product(which, c, q)

            @pl.when(c == 0)
            def _():
                arrived(par, n, q)
                finish(value + recv[par, n, q].astype(F32), q, at)

            @pl.when(c == n - 1)
            def _():
                arrived(par, c, q)
                finish(value + recv[par, c, q].astype(F32), q, at)

            @pl.when((c > 0) & (c < n - 1))
            def _():
                arrived(par, n, q)
                arrived(par, c, q)
                finish(
                    value + recv[par, c, q].astype(F32) + recv[par, n, q].astype(F32), q, at
                )

            return 0

        def finish(value, q, at):
            @pl.when(which == 1)
            def _():
                xsrc[2, at, :] = (value + e_ref[at, :].astype(F32)).astype(BF16)

            @pl.when(which == 0)
            def _():
                abuf[at, :] = value.astype(BF16)
                pair_copy(ex, q).start()

        lax.fori_loop(0, Q, own_step, 0)
        return 0

    products = 2 * ITERS + 1
    lax.fori_loop(0, products, one_product, 0)

    last = ITERS

    def wait_pair(q, _):
        pair_copy(last, q).wait()
        return 0

    lax.fori_loop(0, Q, wait_pair, 0)
    kh = full // 2

    def halves(lo):
        a = abuf[...].astype(F32)
        b = xsrc[last % 2].astype(F32)
        re = jnp.concatenate([a[:, lo : lo + kh], b[:, lo : lo + kh]], axis=1)
        im = jnp.concatenate(
            [a[:, full + lo : full + lo + kh], b[:, full + lo : full + lo + kh]], axis=1
        )
        turn(jnp.concatenate([re, im], axis=1).astype(BF16))

    @pl.when(half == 0)
    def _():
        halves(0)

    @pl.when(half == 1)
    def _():
        halves(kh)

    f_copy.wait()

    def far(d, q):
        at = pl.ds(pl.multiple_of((d * Q + q) * fr, fr), fr)
        field = dot(f[0, at, :], xs[0:rows, :]) + dot(f[1, at, :], xs[rows:, :])
        cosine, sine = cos_ref[at, :], sin_ref[at, :]
        real, imag = field[:, :full], field[:, full:]
        re = cosine * real + sine * imag
        im = cosine * imag - sine * real
        return jnp.concatenate([re[:, :kh] + re[:, kh:], im[:, :kh] + im[:, kh:]], axis=1)

    def far_copy(i, d, q, target, slot_out):
        return pltpu.make_async_remote_copy(
            src_ref=fpart.at[d, q],
            dst_ref=frecv.at[slot_out, q],
            send_sem=fssem.at[i],
            recv_sem=frsem.at[slot_out, q],
            device_id={"col": target},
            device_id_type=MESH,
        )

    def far_arrived(slot, q):
        pltpu.make_async_copy(frecv.at[slot, q], frecv.at[slot, q], frsem.at[slot, q]).wait()

    def far_step(i, _):
        d, q, target, has_in, slot_out = step(i)
        value = far(d, q)

        @pl.when(has_in)
        def _():
            far_arrived(d, q)
            fpart[d, q] = (value + frecv[d, q].astype(F32)).astype(BF16)

        @pl.when(jnp.logical_not(has_in))
        def _():
            fpart[d, q] = value.astype(BF16)

        far_copy(i, d, q, target, slot_out).start()
        return 0

    lax.fori_loop(0, sends, far_step, 0)

    def far_own(q, _):
        at = pl.ds(pl.multiple_of(q * fr, fr), fr)
        out_ref[at, :] = far(c, q)

        @pl.when(c > 0)
        def _():
            far_arrived(c, q)
            out_ref[at, :] += frecv[c, q].astype(F32)

        @pl.when(c < n - 1)
        def _():
            far_arrived(n, q)
            out_ref[at, :] += frecv[n, q].astype(F32)

        return 0

    lax.fori_loop(0, Q, far_own, 0)

    def drain(i, _):
        d, q, target, _, slot_out = step(i)
        send_copy(0, i, d, q, target, slot_out).wait_send()
        send_copy(1, i, d, q, target, slot_out).wait_send()
        far_copy(i, d, q, target, slot_out).wait_send()
        return 0

    lax.fori_loop(0, sends, drain, 0)


def on_device(n, tmatrix, translation, incident, farfield, centres):
    pair_index = lax.axis_index("pair")
    other = jnp.bitwise_xor(pair_index, 2**LEVEL)
    own_incident = incident[0]
    rows, width = own_incident.shape
    total_rows = farfield.shape[1]
    block = total_rows // n
    full = width // 2
    kh = full // 2
    Q = CHUNKS
    spots = jnp.stack(
        [
            lax.dynamic_index_in_dim(centres, pair_index, 0, keepdims=False),
            lax.dynamic_index_in_dim(centres, other, 0, keepdims=False),
        ]
    )
    phases = [direction_phase(spots[m], total_rows) for m in range(2)]

    def lanes(fn):
        return jnp.concatenate(
            [jnp.broadcast_to(fn(phase)[:, None], (total_rows, kh)) for phase in phases], axis=1
        )

    vmem = pl.BlockSpec(memory_space=pltpu.VMEM)
    hbm = pl.BlockSpec(memory_space=pl.ANY)
    dma = pltpu.SemaphoreType.DMA
    out = pl.pallas_call(
        functools.partial(kernel, n),
        out_shape=jax.ShapeDtypeStruct((block, full), F32),
        in_specs=[hbm, hbm, hbm, vmem, vmem, vmem],
        out_specs=vmem,
        scratch_shapes=[
            pltpu.VMEM((2, 2, n * rows, rows), BF16),
            pltpu.VMEM(farfield.shape, BF16),
            pltpu.VMEM((2 * rows, width), BF16),
            pltpu.VMEM((3, rows, width), BF16),
            pltpu.VMEM((rows, width), BF16),
            pltpu.VMEM((2, n, Q, rows // Q, width), BF16),
            pltpu.VMEM((2, n + 1, Q, rows // Q, width), BF16),
            pltpu.VMEM((n, Q, block // Q, full), BF16),
            pltpu.VMEM((n + 1, Q, block // Q, full), BF16),
            dma((2, n * Q)),
            dma,
            dma((2, (n - 1) * Q)),
            dma((2, n + 1, Q)),
            dma((2, Q)),
            dma((2, Q)),
            dma(((n - 1) * Q,)),
            dma((n + 1, Q)),
        ],
        compiler_params=pltpu.CompilerParams(
            collective_id=0, has_side_effects=True, vmem_limit_bytes=63 * 2**20
        ),
    )(tmatrix, translation, farfield, own_incident, lanes(jnp.cos), lanes(jnp.sin))
    return out[None]


def solution(mesh):
    return jax.shard_map(
        functools.partial(on_device, mesh.shape["col"]),
        mesh=mesh,
        in_specs=(
            P("pair", None, None, "col"),
            P("pair", None, None, "col"),
            P("pair", "col", None),
            P(None, None, "col"),
            P(),
        ),
        out_specs=P("pair", "col", None),
        check_vma=False,
    )
```

```python
import functools
import math

import jax
import jax.numpy as jnp
from jax import lax
from jax.experimental import pallas as pl
from jax.experimental.pallas import tpu as pltpu
from jax.sharding import PartitionSpec as P

ITERS = 3
LEVEL = 2
MESH = pl.DeviceIdType.MESH
BF16 = jnp.bfloat16
F32 = jnp.float32
CHUNKS = 4
LAG = 2


def dot(a, b):
    return jnp.dot(a, b, preferred_element_type=F32)


def kernel(
    n, tm, tr, ff, e_hbm, centres, out_ref,
    w, f, e_ref, xs, xsrc, abuf, part, recv, fpart, frecv, trig, cos_ref, sin_ref,
    wsem, fsem, esem, ssem, rsem, psem, qsem, fssem, frsem,
):
    Q = CHUNKS
    c = lax.axis_index("col")
    g = lax.axis_index("pair")
    half = (g // 2**LEVEL) % 2
    other = g + 2**LEVEL * (1 - 2 * half)
    rows, width = e_ref.shape
    full = width // 2
    cr = rows // Q
    fr = out_ref.shape[0] // Q
    sends = (n - 1) * Q

    n_right, n_left = n - 1 - c, c
    prim_right = n_right > n_left
    n_sec = jnp.minimum(n_right, n_left) * Q

    def step(i):
        k = jnp.maximum(i - LAG, 0)
        mid = (i >= LAG) & (k < 2 * n_sec)
        sec = mid & (k % 2 == 0)
        pri_idx = jnp.where(i < LAG, i, jnp.where(mid, LAG + k // 2, i - n_sec))
        idx = jnp.where(sec, k // 2, pri_idx)
        right = jnp.where(sec, jnp.where(prim_right, 0, 1), jnp.where(prim_right, 1, 0))
        j, q = idx // Q, idx % Q
        d = jnp.where(right == 1, n - 1 - j, j)
        target = jnp.where(right == 1, c + 1, c - 1)
        has_in = jnp.where(right == 1, c > 0, c < n - 1)
        slot_out = jnp.where((right == 0) & (d == target), n, d)
        return d, q, target, has_in, slot_out

    def order(i):
        own = i >= sends
        d, q, _, _, _ = step(jnp.minimum(i, sends - 1))
        return jnp.where(own, c, d), jnp.where(own, i - sends, q)

    def w_copy(which, i):
        d, q = order(i)
        src = tm if which == 0 else tr
        at = pl.ds(pl.multiple_of(d * rows + q * cr, cr), cr)
        return pltpu.make_async_copy(src.at[0, :, at, :], w.at[which, :, at, :], wsem.at[which, i])

    e_copy = pltpu.make_async_copy(e_hbm.at[0], e_ref, esem)
    e_copy.start()
    for which in range(2):

        def load(i, _, which=which):
            w_copy(which, i).start()
            return 0

        lax.fori_loop(0, n * Q, load, 0)
    f_copy = pltpu.make_async_copy(ff, f, fsem)
    f_copy.start()

    barrier = pltpu.get_barrier_semaphore()

    @pl.when(c > 0)
    def _():
        pl.semaphore_signal(barrier, inc=1, device_id={"col": c - 1}, device_id_type=MESH)

    @pl.when(c < n - 1)
    def _():
        pl.semaphore_signal(barrier, inc=1, device_id={"col": c + 1}, device_id_type=MESH)

    pl.semaphore_signal(barrier, inc=1, device_id={"pair": other}, device_id_type=MESH)
    pl.semaphore_wait(
        barrier, 1 + jnp.where(c > 0, 1, 0) + jnp.where(c < n - 1, 1, 0)
    )

    def send_copy(par, i, d, q, target, slot_out):
        return pltpu.make_async_remote_copy(
            src_ref=part.at[par, d, q],
            dst_ref=recv.at[par, slot_out, q],
            send_sem=ssem.at[par, i],
            recv_sem=rsem.at[par, slot_out, q],
            device_id={"col": target},
            device_id_type=MESH,
        )

    def arrived(par, slot, q):
        pltpu.make_async_copy(
            recv.at[par, slot, q], recv.at[par, slot, q], rsem.at[par, slot, q]
        ).wait()

    def half_copy(q):
        at = pl.ds(pl.multiple_of(q * cr, cr), cr)
        return pltpu.make_async_remote_copy(
            src_ref=abuf.at[at, 0:full],
            dst_ref=xsrc.at[ITERS % 2, at, 0:full],
            send_sem=psem.at[ITERS % 2, q],
            recv_sem=qsem.at[ITERS % 2, q],
            device_id={"pair": other},
            device_id_type=MESH,
        )

    def pair_copy(ex, q):
        at = pl.ds(pl.multiple_of(q * cr, cr), cr)
        return pltpu.make_async_remote_copy(
            src_ref=abuf.at[at, :],
            dst_ref=xsrc.at[ex % 2, at, :],
            send_sem=psem.at[ex % 2, q],
            recv_sem=qsem.at[ex % 2, q],
            device_id={"pair": other},
            device_id_type=MESH,
        )

    def turn(x):
        xs[0:rows, :] = x
        xs[rows : 2 * rows, 0:full] = -x[:, full:]
        xs[rows : 2 * rows, full:] = x[:, :full]

    def product(which, d, q):
        at = pl.ds(pl.multiple_of(d * rows + q * cr, cr), cr)
        return dot(w[which, 0, at, :], xs[0:rows, :]) + dot(w[which, 1, at, :], xs[rows:, :])

    total_rows = f.shape[1]
    lanes = trig.shape[2]

    def phase_values():
        shape = (total_rows // lanes, lanes)
        s = lax.broadcasted_iota(jnp.int32, shape, 0) * lanes
        s = (s + lax.broadcasted_iota(jnp.int32, shape, 1)).astype(F32)
        polar = math.pi / total_rows * (s + 0.5)
        turns = 40.0 * s
        rest = turns - 97.0 * jnp.floor((turns + 0.5) * (1.0 / 97.0))
        azimuth = 2.0 * math.pi / 97.0 * rest
        ux = jnp.sin(polar) * jnp.cos(azimuth)
        uy = jnp.sin(polar) * jnp.sin(azimuth)
        uz = jnp.cos(polar)
        for m, member in enumerate((g, other)):
            spot = [centres[member, axis].astype(F32) for axis in range(3)]
            phase = 0.7 * (ux * spot[0] + uy * spot[1] + uz * spot[2])
            trig[m] = jnp.cos(phase)
            trig[2 + m] = jnp.sin(phase)

    def spread(r, _):
        at = pl.ds(pl.multiple_of(r * lanes, lanes), lanes)
        for first, table in ((0, cos_ref), (2, sin_ref)):
            both = [
                jnp.broadcast_to(trig[first + m, pl.ds(r, 1), :], (full // 2, lanes))
                for m in range(2)
            ]
            table[at, :] = jnp.concatenate(both, axis=0).T
        return 0

    e_copy.wait()

    last_product = 2 * ITERS
    kh = full // 2

    def one_product(p, _):
        which = p % 2
        par = p % 2
        ex = p // 2

        @pl.when(which == 1)
        def _():
            def wait_pair(q, _):
                pair_copy(ex, q).wait()
                return 0

            lax.fori_loop(0, Q, wait_pair, 0)
            turn(xsrc[ex % 2])

        @pl.when(which == 0)
        def _():
            @pl.when(p == 0)
            def _():
                turn(e_ref[...])

            @pl.when(p > 0)
            def _():
                turn(xsrc[2])

        def loaded(i):
            @pl.when(p == 0)
            def _():
                w_copy(0, i).wait()

            @pl.when(p == 1)
            def _():
                w_copy(1, i).wait()

        def send_step(i, _):
            d, q, target, has_in, slot_out = step(i)
            loaded(i)
            value = product(which, d, q)
            copy = send_copy(par, i, d, q, target, slot_out)

            @pl.when(p >= 2)
            def _():
                copy.wait_send()

            @pl.when(has_in)
            def _():
                arrived(par, d, q)
                part[par, d, q] = (value + recv[par, d, q].astype(F32)).astype(BF16)

            @pl.when(jnp.logical_not(has_in))
            def _():
                part[par, d, q] = value.astype(BF16)

            copy.start()
            return 0

        lax.fori_loop(0, sends, send_step, 0)

        @pl.when(p == 2)
        def _():
            phase_values()

        @pl.when(p == 3)
        def _():
            lax.fori_loop(0, total_rows // lanes, spread, 0)

        def own_step(q, _):
            loaded(sends + q)
            at = pl.ds(pl.multiple_of(q * cr, cr), cr)
            value = product(which, c, q)

            @pl.when(c == 0)
            def _():
                arrived(par, n, q)
                finish(value + recv[par, n, q].astype(F32), q, at)

            @pl.when(c == n - 1)
            def _():
                arrived(par, c, q)
                finish(value + recv[par, c, q].astype(F32), q, at)

            @pl.when((c > 0) & (c < n - 1))
            def _():
                arrived(par, n, q)
                arrived(par, c, q)
                finish(
                    value + recv[par, c, q].astype(F32) + recv[par, n, q].astype(F32), q, at
                )

            return 0

        def finish(value, q, at):
            @pl.when(which == 1)
            def _():
                xsrc[2, at, :] = (value + e_ref[at, :].astype(F32)).astype(BF16)

            @pl.when((which == 0) & (p < last_product))
            def _():
                abuf[at, :] = value.astype(BF16)
                pair_copy(ex, q).start()

            @pl.when(p == last_product)
            def _():
                low = jnp.concatenate([value[:, :kh], value[:, full : full + kh]], axis=1)
                high = jnp.concatenate([value[:, kh:full], value[:, full + kh :]], axis=1)
                abuf[at, 0:full] = jnp.where(half == 0, high, low).astype(BF16)
                abuf[at, full:] = jnp.where(half == 0, low, high).astype(BF16)
                half_copy(q).start()

        lax.fori_loop(0, Q, own_step, 0)
        return 0

    lax.fori_loop(0, last_product + 1, one_product, 0)

    def wait_half(q, _):
        half_copy(q).wait()
        return 0

    lax.fori_loop(0, Q, wait_half, 0)
    own = abuf[:, full:].astype(F32)
    theirs = xsrc[ITERS % 2, :, 0:full].astype(F32)
    turn(
        jnp.concatenate(
            [own[:, :kh], theirs[:, :kh], own[:, kh:], theirs[:, kh:]], axis=1
        ).astype(BF16)
    )
    f_copy.wait()

    def far(d, q):
        at = pl.ds(pl.multiple_of((d * Q + q) * fr, fr), fr)
        field = dot(f[0, at, :], xs[0:rows, :]) + dot(f[1, at, :], xs[rows:, :])
        cosine, sine = cos_ref[at, :], sin_ref[at, :]
        real, imag = field[:, :full], field[:, full:]
        re = cosine * real + sine * imag
        im = cosine * imag - sine * real
        return jnp.concatenate([re[:, :kh] + re[:, kh:], im[:, :kh] + im[:, kh:]], axis=1)

    def far_copy(i, d, q, target, slot_out):
        return pltpu.make_async_remote_copy(
            src_ref=fpart.at[d, q],
            dst_ref=frecv.at[slot_out, q],
            send_sem=fssem.at[i],
            recv_sem=frsem.at[slot_out, q],
            device_id={"col": target},
            device_id_type=MESH,
        )

    def far_arrived(slot, q):
        pltpu.make_async_copy(frecv.at[slot, q], frecv.at[slot, q], frsem.at[slot, q]).wait()

    def far_step(i, _):
        d, q, target, has_in, slot_out = step(i)
        value = far(d, q)

        @pl.when(has_in)
        def _():
            far_arrived(d, q)
            fpart[d, q] = (value + frecv[d, q].astype(F32)).astype(BF16)

        @pl.when(jnp.logical_not(has_in))
        def _():
            fpart[d, q] = value.astype(BF16)

        far_copy(i, d, q, target, slot_out).start()
        return 0

    lax.fori_loop(0, sends, far_step, 0)

    def far_own(q, _):
        at = pl.ds(pl.multiple_of(q * fr, fr), fr)
        out_ref[at, :] = far(c, q)

        @pl.when(c > 0)
        def _():
            far_arrived(c, q)
            out_ref[at, :] += frecv[c, q].astype(F32)

        @pl.when(c < n - 1)
        def _():
            far_arrived(n, q)
            out_ref[at, :] += frecv[n, q].astype(F32)

        return 0

    lax.fori_loop(0, Q, far_own, 0)

    def drain(i, _):
        d, q, target, _, slot_out = step(i)
        send_copy(0, i, d, q, target, slot_out).wait_send()
        send_copy(1, i, d, q, target, slot_out).wait_send()
        far_copy(i, d, q, target, slot_out).wait_send()
        return 0

    lax.fori_loop(0, sends, drain, 0)


def on_device(n, tmatrix, translation, incident, farfield, centres):
    _, rows, width = incident.shape
    total_rows = farfield.shape[1]
    block = total_rows // n
    full = width // 2
    Q = CHUNKS
    vmem = pl.BlockSpec(memory_space=pltpu.VMEM)
    hbm = pl.BlockSpec(memory_space=pl.ANY)
    dma = pltpu.SemaphoreType.DMA
    out = pl.pallas_call(
        functools.partial(kernel, n),
        out_shape=jax.ShapeDtypeStruct((block, full), F32),
        in_specs=[hbm, hbm, hbm, hbm, pl.BlockSpec(memory_space=pltpu.SMEM)],
        out_specs=vmem,
        scratch_shapes=[
            pltpu.VMEM((2, 2, n * rows, rows), BF16),
            pltpu.VMEM(farfield.shape, BF16),
            pltpu.VMEM((rows, width), BF16),
            pltpu.VMEM((2 * rows, width), BF16),
            pltpu.VMEM((3, rows, width), BF16),
            pltpu.VMEM((rows, width), BF16),
            pltpu.VMEM((2, n, Q, rows // Q, width), BF16),
            pltpu.VMEM((2, n + 1, Q, rows // Q, width), BF16),
            pltpu.VMEM((n, Q, block // Q, full), BF16),
            pltpu.VMEM((n + 1, Q, block // Q, full), BF16),
            pltpu.VMEM((4, total_rows // 128, 128), F32),
            pltpu.VMEM((total_rows, full), F32),
            pltpu.VMEM((total_rows, full), F32),
            dma((2, n * Q)),
            dma,
            dma,
            dma((2, (n - 1) * Q)),
            dma((2, n + 1, Q)),
            dma((2, Q)),
            dma((2, Q)),
            dma(((n - 1) * Q,)),
            dma((n + 1, Q)),
        ],
        compiler_params=pltpu.CompilerParams(
            collective_id=0, has_side_effects=True, vmem_limit_bytes=63 * 2**20
        ),
    )(tmatrix, translation, farfield, incident, centres)
    return out[None]


def solution(mesh):
    return jax.shard_map(
        functools.partial(on_device, mesh.shape["col"]),
        mesh=mesh,
        in_specs=(
            P("pair", None, None, "col"),
            P("pair", None, None, "col"),
            P("pair", "col", None),
            P(None, None, "col"),
            P(),
        ),
        out_specs=P("pair", "col", None),
        check_vma=False,
    )
```

```python
import functools
import math

import jax
import jax.numpy as jnp
from jax import lax
from jax.experimental import pallas as pl
from jax.experimental.pallas import tpu as pltpu
from jax.sharding import PartitionSpec as P

ITERS = 3
LEVEL = 2
MESH = pl.DeviceIdType.MESH
BF16 = jnp.bfloat16
F32 = jnp.float32
CHUNKS = 4
LAG = 4


def dot(a, b):
    return jnp.dot(a, b, preferred_element_type=F32)


def kernel(
    n, tm, tr, ff, e_hbm, centres, out_ref,
    w, f, e_ref, xs, xsrc, abuf, part, recv, fpart, frecv, trig, cos_ref, sin_ref,
    wsem, fsem, esem, ssem, rsem, psem, qsem, fssem, frsem,
):
    Q = CHUNKS
    c = lax.axis_index("col")
    g = lax.axis_index("pair")
    half = (g // 2**LEVEL) % 2
    other = g + 2**LEVEL * (1 - 2 * half)
    rows, width = e_ref.shape
    full = width // 2
    cr = rows // Q
    fr = out_ref.shape[0] // Q
    sends = (n - 1) * Q

    n_right, n_left = n - 1 - c, c
    prim_right = n_right > n_left
    n_sec = jnp.minimum(n_right, n_left) * Q

    def step(i):
        k = jnp.maximum(i - LAG, 0)
        mid = (i >= LAG) & (k < 2 * n_sec)
        sec = mid & (k % 2 == 0)
        pri_idx = jnp.where(i < LAG, i, jnp.where(mid, LAG + k // 2, i - n_sec))
        idx = jnp.where(sec, k // 2, pri_idx)
        right = jnp.where(sec, jnp.where(prim_right, 0, 1), jnp.where(prim_right, 1, 0))
        j, q = idx // Q, idx % Q
        d = jnp.where(right == 1, n - 1 - j, j)
        target = jnp.where(right == 1, c + 1, c - 1)
        has_in = jnp.where(right == 1, c > 0, c < n - 1)
        slot_out = jnp.where((right == 0) & (d == target), n, d)
        return d, q, target, has_in, slot_out

    def order(i):
        own = i >= sends
        d, q, _, _, _ = step(jnp.minimum(i, sends - 1))
        return jnp.where(own, c, d), jnp.where(own, i - sends, q)

    def w_copy(which, i):
        d, q = order(i)
        src = tm if which == 0 else tr
        at = pl.ds(pl.multiple_of(d * rows + q * cr, cr), cr)
        return pltpu.make_async_copy(src.at[0, :, at, :], w.at[which, :, at, :], wsem.at[which, i])

    e_copy = pltpu.make_async_copy(e_hbm.at[0], e_ref, esem)
    e_copy.start()
    for which in range(2):

        def load(i, _, which=which):
            w_copy(which, i).start()
            return 0

        lax.fori_loop(0, n * Q, load, 0)
    f_copy = pltpu.make_async_copy(ff, f, fsem)
    f_copy.start()

    barrier = pltpu.get_barrier_semaphore()

    @pl.when(c > 0)
    def _():
        pl.semaphore_signal(barrier, inc=1, device_id={"col": c - 1}, device_id_type=MESH)

    @pl.when(c < n - 1)
    def _():
        pl.semaphore_signal(barrier, inc=1, device_id={"col": c + 1}, device_id_type=MESH)

    pl.semaphore_signal(barrier, inc=1, device_id={"pair": other}, device_id_type=MESH)
    pl.semaphore_wait(
        barrier, 1 + jnp.where(c > 0, 1, 0) + jnp.where(c < n - 1, 1, 0)
    )

    def send_copy(par, i, d, q, target, slot_out):
        return pltpu.make_async_remote_copy(
            src_ref=part.at[par, d, q],
            dst_ref=recv.at[par, slot_out, q],
            send_sem=ssem.at[par, i],
            recv_sem=rsem.at[par, slot_out, q],
            device_id={"col": target},
            device_id_type=MESH,
        )

    def arrived(par, slot, q):
        pltpu.make_async_copy(
            recv.at[par, slot, q], recv.at[par, slot, q], rsem.at[par, slot, q]
        ).wait()

    def half_copy(q):
        at = pl.ds(pl.multiple_of(q * cr, cr), cr)
        return pltpu.make_async_remote_copy(
            src_ref=abuf.at[at, 0:full],
            dst_ref=xsrc.at[ITERS % 2, at, 0:full],
            send_sem=psem.at[ITERS % 2, q],
            recv_sem=qsem.at[ITERS % 2, q],
            device_id={"pair": other},
            device_id_type=MESH,
        )

    def pair_copy(ex, q):
        at = pl.ds(pl.multiple_of(q * cr, cr), cr)
        return pltpu.make_async_remote_copy(
            src_ref=abuf.at[at, :],
            dst_ref=xsrc.at[ex % 2, at, :],
            send_sem=psem.at[ex % 2, q],
            recv_sem=qsem.at[ex % 2, q],
            device_id={"pair": other},
            device_id_type=MESH,
        )

    def turn(x):
        xs[0:rows, :] = x
        xs[rows : 2 * rows, 0:full] = -x[:, full:]
        xs[rows : 2 * rows, full:] = x[:, :full]

    def turn_chunk(x, q):
        at = pl.ds(pl.multiple_of(q * cr, cr), cr)
        below = pl.ds(pl.multiple_of(rows + q * cr, cr), cr)
        xs[at, :] = x
        xs[below, 0:full] = -x[:, full:]
        xs[below, full:] = x[:, :full]

    def product(which, d, q):
        at = pl.ds(pl.multiple_of(d * rows + q * cr, cr), cr)
        return dot(w[which, 0, at, :], xs[0:rows, :]) + dot(w[which, 1, at, :], xs[rows:, :])

    total_rows = f.shape[1]
    lanes = trig.shape[2]

    def phase_values():
        shape = (total_rows // lanes, lanes)
        s = lax.broadcasted_iota(jnp.int32, shape, 0) * lanes
        s = (s + lax.broadcasted_iota(jnp.int32, shape, 1)).astype(F32)
        polar = math.pi / total_rows * (s + 0.5)
        turns = 40.0 * s
        rest = turns - 97.0 * jnp.floor((turns + 0.5) * (1.0 / 97.0))
        azimuth = 2.0 * math.pi / 97.0 * rest
        ux = jnp.sin(polar) * jnp.cos(azimuth)
        uy = jnp.sin(polar) * jnp.sin(azimuth)
        uz = jnp.cos(polar)
        for m, member in enumerate((g, other)):
            spot = [centres[member, axis].astype(F32) for axis in range(3)]
            phase = 0.7 * (ux * spot[0] + uy * spot[1] + uz * spot[2])
            trig[m] = jnp.cos(phase)
            trig[2 + m] = jnp.sin(phase)

    def spread(r, _):
        at = pl.ds(pl.multiple_of(r * lanes, lanes), lanes)
        for first, table in ((0, cos_ref), (2, sin_ref)):
            both = [
                jnp.broadcast_to(trig[first + m, pl.ds(r, 1), :], (full // 2, lanes))
                for m in range(2)
            ]
            table[at, :] = jnp.concatenate(both, axis=0).T
        return 0

    e_copy.wait()

    last_product = 2 * ITERS
    kh = full // 2

    def one_product(p, _):
        which = p % 2
        par = p % 2
        ex = p // 2

        @pl.when(which == 1)
        def _():
            def wait_pair(q, _):
                pair_copy(ex, q).wait()
                turn_chunk(xsrc[ex % 2, pl.ds(pl.multiple_of(q * cr, cr), cr), :], q)
                return 0

            lax.fori_loop(0, Q, wait_pair, 0)

        @pl.when(which == 0)
        def _():
            @pl.when(p == 0)
            def _():
                turn(e_ref[...])

            @pl.when(p > 0)
            def _():
                turn(xsrc[2])

        def loaded(i):
            @pl.when(p == 0)
            def _():
                w_copy(0, i).wait()

            @pl.when(p == 1)
            def _():
                w_copy(1, i).wait()

        def send_step(i, _):
            d, q, target, has_in, slot_out = step(i)
            loaded(i)
            value = product(which, d, q)
            copy = send_copy(par, i, d, q, target, slot_out)

            @pl.when(p >= 2)
            def _():
                copy.wait_send()

            @pl.when(has_in)
            def _():
                arrived(par, d, q)
                part[par, d, q] = (value + recv[par, d, q].astype(F32)).astype(BF16)

            @pl.when(jnp.logical_not(has_in))
            def _():
                part[par, d, q] = value.astype(BF16)

            copy.start()
            return 0

        lax.fori_loop(0, sends, send_step, 0)

        @pl.when(p == 2)
        def _():
            phase_values()

        @pl.when(p == 3)
        def _():
            lax.fori_loop(0, total_rows // lanes, spread, 0)

        def own_step(q, _):
            loaded(sends + q)
            at = pl.ds(pl.multiple_of(q * cr, cr), cr)
            value = product(which, c, q)

            @pl.when(c == 0)
            def _():
                arrived(par, n, q)
                finish(value + recv[par, n, q].astype(F32), q, at)

            @pl.when(c == n - 1)
            def _():
                arrived(par, c, q)
                finish(value + recv[par, c, q].astype(F32), q, at)

            @pl.when((c > 0) & (c < n - 1))
            def _():
                arrived(par, n, q)
                arrived(par, c, q)
                finish(
                    value + recv[par, c, q].astype(F32) + recv[par, n, q].astype(F32), q, at
                )

            return 0

        def finish(value, q, at):
            @pl.when(which == 1)
            def _():
                xsrc[2, at, :] = (value + e_ref[at, :].astype(F32)).astype(BF16)

            @pl.when((which == 0) & (p < last_product))
            def _():
                abuf[at, :] = value.astype(BF16)
                pair_copy(ex, q).start()

            @pl.when(p == last_product)
            def _():
                low = jnp.concatenate([value[:, :kh], value[:, full : full + kh]], axis=1)
                high = jnp.concatenate([value[:, kh:full], value[:, full + kh :]], axis=1)
                abuf[at, 0:full] = jnp.where(half == 0, high, low).astype(BF16)
                abuf[at, full:] = jnp.where(half == 0, low, high).astype(BF16)
                half_copy(q).start()

        lax.fori_loop(0, Q, own_step, 0)
        return 0

    lax.fori_loop(0, last_product + 1, one_product, 0)

    def wait_half(q, _):
        half_copy(q).wait()
        at = pl.ds(pl.multiple_of(q * cr, cr), cr)
        own = abuf[at, full:].astype(F32)
        theirs = xsrc[ITERS % 2, at, 0:full].astype(F32)
        sides = [own[:, :kh], theirs[:, :kh], own[:, kh:], theirs[:, kh:]]
        turn_chunk(jnp.concatenate(sides, axis=1).astype(BF16), q)
        return 0

    lax.fori_loop(0, Q, wait_half, 0)
    f_copy.wait()

    def far(d, q):
        at = pl.ds(pl.multiple_of((d * Q + q) * fr, fr), fr)
        field = dot(f[0, at, :], xs[0:rows, :]) + dot(f[1, at, :], xs[rows:, :])
        cosine, sine = cos_ref[at, :], sin_ref[at, :]
        real, imag = field[:, :full], field[:, full:]
        re = cosine * real + sine * imag
        im = cosine * imag - sine * real
        return jnp.concatenate([re[:, :kh] + re[:, kh:], im[:, :kh] + im[:, kh:]], axis=1)

    def far_copy(i, d, q, target, slot_out):
        return pltpu.make_async_remote_copy(
            src_ref=fpart.at[d, q],
            dst_ref=frecv.at[slot_out, q],
            send_sem=fssem.at[i],
            recv_sem=frsem.at[slot_out, q],
            device_id={"col": target},
            device_id_type=MESH,
        )

    def far_arrived(slot, q):
        pltpu.make_async_copy(frecv.at[slot, q], frecv.at[slot, q], frsem.at[slot, q]).wait()

    def far_step(i, _):
        d, q, target, has_in, slot_out = step(i)
        value = far(d, q)

        @pl.when(has_in)
        def _():
            far_arrived(d, q)
            fpart[d, q] = (value + frecv[d, q].astype(F32)).astype(BF16)

        @pl.when(jnp.logical_not(has_in))
        def _():
            fpart[d, q] = value.astype(BF16)

        far_copy(i, d, q, target, slot_out).start()
        return 0

    lax.fori_loop(0, sends, far_step, 0)

    def far_own(q, _):
        at = pl.ds(pl.multiple_of(q * fr, fr), fr)
        out_ref[at, :] = far(c, q)

        @pl.when(c > 0)
        def _():
            far_arrived(c, q)
            out_ref[at, :] += frecv[c, q].astype(F32)

        @pl.when(c < n - 1)
        def _():
            far_arrived(n, q)
            out_ref[at, :] += frecv[n, q].astype(F32)

        return 0

    lax.fori_loop(0, Q, far_own, 0)

    def drain(i, _):
        d, q, target, _, slot_out = step(i)
        send_copy(0, i, d, q, target, slot_out).wait_send()
        send_copy(1, i, d, q, target, slot_out).wait_send()
        far_copy(i, d, q, target, slot_out).wait_send()
        return 0

    lax.fori_loop(0, sends, drain, 0)


def on_device(n, tmatrix, translation, incident, farfield, centres):
    _, rows, width = incident.shape
    total_rows = farfield.shape[1]
    block = total_rows // n
    full = width // 2
    Q = CHUNKS
    vmem = pl.BlockSpec(memory_space=pltpu.VMEM)
    hbm = pl.BlockSpec(memory_space=pl.ANY)
    dma = pltpu.SemaphoreType.DMA
    out = pl.pallas_call(
        functools.partial(kernel, n),
        out_shape=jax.ShapeDtypeStruct((block, full), F32),
        in_specs=[hbm, hbm, hbm, hbm, pl.BlockSpec(memory_space=pltpu.SMEM)],
        out_specs=vmem,
        scratch_shapes=[
            pltpu.VMEM((2, 2, n * rows, rows), BF16),
            pltpu.VMEM(farfield.shape, BF16),
            pltpu.VMEM((rows, width), BF16),
            pltpu.VMEM((2 * rows, width), BF16),
            pltpu.VMEM((3, rows, width), BF16),
            pltpu.VMEM((rows, width), BF16),
            pltpu.VMEM((2, n, Q, rows // Q, width), BF16),
            pltpu.VMEM((2, n + 1, Q, rows // Q, width), BF16),
            pltpu.VMEM((n, Q, block // Q, full), BF16),
            pltpu.VMEM((n + 1, Q, block // Q, full), BF16),
            pltpu.VMEM((4, total_rows // 128, 128), F32),
            pltpu.VMEM((total_rows, full), F32),
            pltpu.VMEM((total_rows, full), F32),
            dma((2, n * Q)),
            dma,
            dma,
            dma((2, (n - 1) * Q)),
            dma((2, n + 1, Q)),
            dma((2, Q)),
            dma((2, Q)),
            dma(((n - 1) * Q,)),
            dma((n + 1, Q)),
        ],
        compiler_params=pltpu.CompilerParams(
            collective_id=0, has_side_effects=True, vmem_limit_bytes=63 * 2**20
        ),
    )(tmatrix, translation, farfield, incident, centres)
    return out[None]


def solution(mesh):
    return jax.shard_map(
        functools.partial(on_device, mesh.shape["col"]),
        mesh=mesh,
        in_specs=(
            P("pair", None, None, "col"),
            P("pair", None, None, "col"),
            P("pair", "col", None),
            P(None, None, "col"),
            P(),
        ),
        out_specs=P("pair", "col", None),
        check_vma=False,
    )
```
